128 devices in a mesh: section: 4 (over x), dom: 32 (over y, z, core).
Axes of the slice: x: 4, y: 4, z: 4, core: 2. Of those that a mesh axis runs over, the one named last changes fastest.
Arguments:
- h0: bfloat16 [2, 49152, 512], P(None, 'dom'), may hold values from -6 to 6
- layer_weight: bfloat16 [8, 512, 512], P('section'), may hold values from -0.25 to 0.25
- tile_vals: bfloat16 [2, 384, 4, 128, 128], P(None, 'dom'), may hold values from -0.375 to 0.375
- tile_cols: int32 [2, 384, 4], P(None, 'dom'), may hold values from 0 to 13, as said below
- boundary: int32 [2, 1024], P(None, 'dom'), may hold values from 0 to 1535
- send_pos: int32 [2, 1024, 8], P(None, 'dom'), may hold values from 0 to 31
- send_count: int32 [2, 1024], P(None, 'dom'), may hold values from 0 to 8, as said below
Outputs:
- section_out: bfloat16 [4, 2, 49152, 512], P('section', None, 'dom')
The draws below stay inside these ranges and needn't reach their ends.
Inputs may be any that keep to these rules, and one draw needn't show every extreme that they name: `tile_cols`: each partition's row of tiles names its own diagonal tile first; tiles 12 and up are the received rows. `send_count`: zero from a partition to itself; in every batch each partition p sends 8 live slots to partition p + 1 (mod 32).
All inputs are finite; a program needn't handle non-finite values.
Results may differ from the reference program's by a relative error of at most 0.014.
Values may be sent and summed in bfloat16 or wider, within the bound.
No kernel may reach another device: no remote copies, remote signals or barrier semaphores. Data moves between devices by JAX's collectives and lax.ppermute only.
A program may use at most 128 MiB of HBM per device.

```python
import math
import jax
import jax.numpy as jnp
from jax import lax

D = 512
NODE_DEV = 1536
BATCHES = 2
L_ST = 2
TILE = 128
KT = 4
BOUND = 32
CAP = 8
LAYERS = 8
NODES = 49152
ROW_TILES = 12
HALO_TILES = 2
COL_TILES = 14
ALL_ROW_TILES = 384
N_SECTION = 4
N_DOM = 32


def draw_send_count(key, part):
    counts = jax.random.randint(key, (BATCHES, N_DOM, N_DOM), 1, CAP + 1)
    sender = jnp.arange(N_DOM, dtype=jnp.int32)[:, None]
    target = jnp.arange(N_DOM, dtype=jnp.int32)[None, :]
    counts = jnp.where(target == (sender + 1) % N_DOM, CAP, counts)
    counts = jnp.where(target == sender, 0, counts)
    return counts.reshape(BATCHES, N_DOM * N_DOM).astype(jnp.int32)


def draw_tile_cols(key, part):
    first_key = jax.random.fold_in(key, 11)
    second_key = jax.random.fold_in(key, 23)
    row_pos = jnp.broadcast_to(jnp.arange(ROW_TILES, dtype=jnp.int32), (BATCHES, N_DOM, ROW_TILES))
    shift_local = jax.random.randint(first_key, (BATCHES, N_DOM, ROW_TILES), 0, max(ROW_TILES - 1, 1))
    shift_halo = jax.random.randint(second_key, (BATCHES, N_DOM, ROW_TILES), 0, max(HALO_TILES - 1, 1))
    other_local = (row_pos + 1 + shift_local) % ROW_TILES
    halo_first = row_pos % HALO_TILES
    halo_second = (halo_first + 1 + shift_halo) % HALO_TILES
    stacked = jnp.stack([row_pos, ROW_TILES + halo_first, other_local, ROW_TILES + halo_second], -1)
    return stacked.reshape(BATCHES, N_DOM * ROW_TILES, KT).astype(jnp.int32)


def place_ends(array, rng, smallest, high):
    longest = array.shape.index(max(array.shape))
    spots = []
    for shift in (0, 1):
        where = [jax.random.randint(jax.random.fold_in(rng, axis), (), 0, length) for axis, length in enumerate(array.shape)]
        where[longest] = (where[longest] + shift) % array.shape[longest]
        spots.append(tuple(where))
    return array.at[spots[0]].set(smallest).at[spots[1]].set(high)


def levels(rng, dims, pieces, least, high):
    level = 1.0
    for position, shards_of in pieces:
        steps = jax.random.uniform(jax.random.fold_in(jax.random.fold_in(rng, 6), position), (shards_of,), jnp.float32, least / len(pieces), high / len(pieces))
        level = level * jnp.repeat(jnp.exp(steps), dims[position] // shards_of).reshape((-1,) + (1,) * (len(dims) - 1 - position))
    return level


def gaussian(stream_key, extent, spread, most, split=(), kind=jnp.bfloat16):
    factor_of = levels(stream_key, extent, split, -0.22, 0.18) if split else 1.0
    result = jax.random.normal(stream_key, extent, jnp.float32) * spread * factor_of
    return jnp.minimum(jnp.maximum(result, -most), most).astype(kind)


def setup_inputs(seed: int = 0) -> dict:
    keys = jax.random.split(jax.random.key(seed), 8)
    return {
        "h0": gaussian(keys[0], (BATCHES, NODES, D), 1.0, 6.0, ((1, 32),)),
        "layer_weight": gaussian(keys[1], (LAYERS, D, D), D ** -0.5, 0.25, ((0, 4),)),
        "tile_vals": gaussian(keys[2], (BATCHES, ALL_ROW_TILES, KT, TILE, TILE), (KT * TILE // 2) ** -0.5, 0.375, ((1, 32),)),
        "tile_cols": draw_tile_cols(jax.random.fold_in(keys[7], 71), 0),
        "boundary": place_ends(jax.random.randint(keys[4], (BATCHES, N_DOM * BOUND), 0, NODE_DEV), jax.random.fold_in(keys[4], 1), 0, NODE_DEV - 1).astype(jnp.int32),
        "send_pos": place_ends(jax.random.randint(keys[5], (BATCHES, N_DOM * N_DOM, CAP), 0, BOUND), jax.random.fold_in(keys[5], 1), 0, BOUND - 1).astype(jnp.int32),
        "send_count": draw_send_count(jax.random.fold_in(keys[7], 71), 0),
    }


restart_share = 0.1
decay_scale = 1.0


def one_partition(args, weight, layer_beta):
    features, received, starting, tile_block, column_ids = args
    spare = jnp.zeros((HALO_TILES * TILE - N_DOM * CAP, D), features.dtype)
    table = jnp.concatenate([features, received, spare], 0).reshape(COL_TILES, TILE, D)
    blocks = table[column_ids]
    mixed = jnp.einsum("rkij,rkjd->rid", tile_block.astype(jnp.float32), blocks.astype(jnp.float32)).reshape(NODE_DEV, D)
    zvalue = (1.0 - restart_share) * mixed + restart_share * starting.astype(jnp.float32)
    zround = zvalue.astype(jnp.bfloat16)
    product = jnp.dot(zround, weight, preferred_element_type=jnp.float32)
    return jax.nn.relu((1.0 - layer_beta) * zvalue + layer_beta * product).astype(jnp.bfloat16)


def reference(h0, layer_weight, tile_vals, tile_cols, boundary, send_pos, send_count):
    per_batch = []
    for batch_no in range(BATCHES):
        bound_rows = boundary[batch_no].reshape(N_DOM, BOUND)
        positions = send_pos[batch_no].reshape(N_DOM, N_DOM * CAP)
        local_idx = jnp.take_along_axis(bound_rows, positions, axis=1).reshape(N_DOM, N_DOM, CAP)
        global_idx = local_idx + (jnp.arange(N_DOM, dtype=jnp.int32) * NODE_DEV)[:, None, None]
        live = jnp.arange(CAP, dtype=jnp.int32)[None, None, :] < send_count[batch_no].reshape(N_DOM, N_DOM)[:, :, None]
        tile_block = tile_vals[batch_no].reshape(N_DOM, ROW_TILES, KT, TILE, TILE)
        column_ids = tile_cols[batch_no].reshape(N_DOM, ROW_TILES, KT).astype(jnp.int32)
        starting = h0[batch_no].reshape(N_DOM, NODE_DEV, D)
        current = h0[batch_no]
        section_list = []
        for section_no in range(N_SECTION):
            for inner in range(L_ST):
                layer_no = section_no * L_ST + inner
                layer_beta = math.log(decay_scale / (layer_no + 1) + 1.0)
                gathered = current[global_idx]
                gathered = jnp.where(live[..., None], gathered, jnp.zeros_like(gathered))
                received = jnp.transpose(gathered, (1, 0, 2, 3)).reshape(N_DOM, N_DOM * CAP, D)
                weight = layer_weight[layer_no]
                current = lax.map(lambda args: one_partition(args, weight, layer_beta),
                                  (current.reshape(N_DOM, NODE_DEV, D), received, starting, tile_block, column_ids))
                current = current.reshape(NODES, D)
            section_list.append(current)
        per_batch.append(jnp.stack(section_list, 0))
    return jnp.stack(per_batch, 1)
```

```python
import math
import jax
import jax.numpy as jnp
from jax import lax
from jax.experimental import pallas as pl
from jax.experimental.pallas import tpu as pltpu
from jax.sharding import PartitionSpec as P

restart_share = 0.1
decay_scale = 1.0
f32 = jnp.float32
bf16 = jnp.bfloat16


def dot(a, b):
    return jnp.dot(a, b, preferred_element_type=f32)


def whole(*shape):
    return pl.BlockSpec(shape, lambda: (0,) * len(shape))


def pick_kernel(h0_ref, rows_ref, slots_ref, send_ref, picked_ref):
    batches, bound, _ = rows_ref.shape
    picked = []
    for b in range(batches):
        picked.append(dot(rows_ref[b], h0_ref[b]))
    picked = jnp.concatenate(picked, 0)
    picked_ref[...] = restart_share * picked
    send_ref[...] = dot(slots_ref[...], picked.astype(bf16)).astype(bf16)


def spread_of(b, batches, rows, cap):
    row = lax.broadcasted_iota(jnp.int32, (rows, rows * batches), 0)
    col = lax.broadcasted_iota(jnp.int32, (rows, rows * batches), 1)
    hit = col == (row // cap) * (cap * batches) + b * cap + row % cap
    return jnp.where(hit, 1.0, 0.0).astype(bf16)


def bound_kernel(cap, cols_ref, h0_ref, rows_ref, vals_ref, picked_ref, local_ref, halo_ref, part_ref, acc_ref):
    batches, bound, nodes = rows_ref.shape
    _, row_tiles, kt, tile, _ = vals_ref.shape
    halo = halo_ref.shape[1] // batches
    for b in range(batches):
        acc_ref[...] = jnp.zeros_like(acc_ref)
        for r in range(row_tiles):
            sel = rows_ref[b, :, r * tile:(r + 1) * tile]
            for k in range(kt):
                c = cols_ref[(b * row_tiles + r) * kt + k]
                acc_ref[c] += dot(sel, vals_ref[b, r, k])
        local = jnp.concatenate([acc_ref[t] for t in range(row_tiles)], 1).astype(bf16)
        rest = jnp.concatenate([acc_ref[t] for t in range(row_tiles, acc_ref.shape[0])], 1).astype(bf16)
        local_ref[b] = local
        halo_ref[b * bound:(b + 1) * bound, :] = dot(rest, spread_of(b, batches, halo, cap)).astype(bf16)
        part_ref[b * bound:(b + 1) * bound, :] = (
            (1.0 - restart_share) * dot(local, h0_ref[b]) + picked_ref[b * bound:(b + 1) * bound, :])


def edge_kernel(beta, part_ref, halo_ref, recv_ref, w_ref, slots_ref, send_ref):
    z = part_ref[...] + (1.0 - restart_share) * dot(halo_ref[...], recv_ref[...])
    prod = dot(z.astype(bf16), w_ref[...])
    h = jnp.maximum((1.0 - beta) * z + beta * prod, 0.0).astype(bf16)
    send_ref[...] = dot(slots_ref[...], h).astype(bf16)


def bulk_kernel(beta, first_live, cap, meta_ref, x_ref, recv_ref, vals_ref, h0_ref, w_ref, local_ref, picked_ref,
                h_ref, part_ref, table_ref):
    b, g = pl.program_id(0), pl.program_id(1)
    batches = pl.num_programs(0)
    _, tiles, kt, tile, _ = vals_ref.shape
    row_tiles = tiles * pl.num_programs(1)
    nodes = x_ref.shape[1]
    rows = tiles * tile
    live = meta_ref[0] >= first_live

    @pl.when(jnp.logical_not(live))
    def _():
        h_ref[0] = x_ref[0, pl.ds(pl.multiple_of(g * rows, rows), rows), :]
        part_ref[...] = jnp.zeros_like(part_ref)

    @pl.when(live & (g == 0))
    def _():
        for t in range(nodes // tile):
            table_ref[t] = x_ref[0, t * tile:(t + 1) * tile, :]
        halo = table_ref.shape[0] * tile - nodes
        spread = spread_of(b, recv_ref.shape[0] // halo, halo, cap)
        got = dot(spread, recv_ref[...]).astype(bf16)
        for t in range(halo // tile):
            table_ref[nodes // tile + t] = got[t * tile:(t + 1) * tile]
        part_ref[0] = picked_ref[0]

    @pl.when(live)
    def _():
        zs = []
        for r in range(tiles):
            base = 1 + (b * row_tiles + g * tiles + r) * kt
            lhs = jnp.concatenate([vals_ref[0, r, k] for k in range(kt)], 1)
            rhs = jnp.concatenate([table_ref[meta_ref[base + k]] for k in range(kt)], 0)
            zs.append(dot(lhs, rhs))
        z = (1.0 - restart_share) * jnp.concatenate(zs, 0) + restart_share * h0_ref[0].astype(f32)
        prod = dot(z.astype(bf16), w_ref[...])
        h = jnp.maximum((1.0 - beta) * z + beta * prod, 0.0).astype(bf16)
        h_ref[0] = h
        part_ref[0] += (1.0 - restart_share) * dot(local_ref[0], h)


def params(**kw):
    return pltpu.CompilerParams(vmem_limit_bytes=28 * 1024 * 1024, **kw)


def cost(flops, nbytes):
    return pl.CostEstimate(flops=int(flops), bytes_accessed=int(nbytes), transcendentals=0)


def body(h0, layer_weight, tile_vals, tile_cols, boundary, send_pos, send_count):
    sections = lax.axis_size("section")
    place = lax.axis_index("section").astype(jnp.int32)
    batches, nodes, width = h0.shape
    depth = layer_weight.shape[0]
    layers = depth * sections
    _, row_tiles, kt, tile, _ = tile_vals.shape
    bound = boundary.shape[1]
    doms, cap = send_pos.shape[1], send_pos.shape[2]
    halo = doms * cap
    all_tiles = (nodes + halo + tile - 1) // tile
    groups = 3
    rows = nodes // groups

    turned = [[layer_weight[i] for i in range(depth)]]
    for i in range(depth):
        for k in range(1, sections):
            if i == 0:
                turned.append([None] * depth)
            turned[k][i] = lax.ppermute(layer_weight[i], "section", [(s, (s + k) % sections) for s in range(sections)])

    def weight_of(layer):
        s, i = layer // depth, layer % depth
        turn = (place - s) % sections
        w = turned[0][i]
        for k in range(1, sections):
            w = jnp.where(turn == k, turned[k][i], w)
        return w

    node_id = jnp.arange(nodes, dtype=jnp.int32)
    rows_sel = (boundary[:, :, None] == node_id[None, None, :]).astype(bf16)
    live = jnp.arange(cap, dtype=jnp.int32)[None, None, :] < send_count[:, :, None]
    slot = jnp.where(live, send_pos + bound * jnp.arange(batches, dtype=jnp.int32)[:, None, None], -1)
    slot = jnp.transpose(slot, (1, 0, 2)).reshape(doms * batches * cap)
    slots_sel = (slot[:, None] == jnp.arange(batches * bound, dtype=jnp.int32)[None, :]).astype(bf16)
    cols = tile_cols.reshape(-1).astype(jnp.int32)
    meta = jnp.concatenate([place[None], cols])

    lines = doms * batches * cap

    def exchanged(x):
        return lax.all_to_all(x, "dom", split_axis=0, concat_axis=0, tiled=True)

    send, picked = pl.pallas_call(
        pick_kernel,
        out_shape=(jax.ShapeDtypeStruct((lines, width), bf16), jax.ShapeDtypeStruct((batches * bound, width), f32)),
        compiler_params=params(),
        name="pick",
    )(h0, rows_sel, slots_sel)
    recv = exchanged(send)

    local, halo_sel, part = pl.pallas_call(
        lambda *refs: bound_kernel(cap, *refs),
        in_specs=[pl.BlockSpec(memory_space=pltpu.SMEM)] + [pl.BlockSpec(memory_space=pltpu.VMEM)] * 4,
        out_shape=(
            jax.ShapeDtypeStruct((batches, bound, nodes), bf16),
            jax.ShapeDtypeStruct((batches * bound, lines), bf16),
            jax.ShapeDtypeStruct((batches * bound, width), f32),
        ),
        scratch_shapes=[pltpu.VMEM((all_tiles, bound, tile), f32)],
        compiler_params=params(),
        cost_estimate=cost(4e9, 8e6),
        name="bound",
    )(cols, h0, rows_sel, tile_vals, picked)
    picked3 = picked.reshape(batches, bound, width)

    def edge(part, recv, w, beta):
        return pl.pallas_call(
            lambda *refs: edge_kernel(beta, *refs),
            out_shape=jax.ShapeDtypeStruct((lines, width), bf16),
            compiler_params=params(),
            cost_estimate=cost(1e8, 2e6),
            name="edge",
        )(part, halo_sel, recv, w, slots_sel)

    def bulk(x, recv, w, beta, first_live):
        h, part = pl.pallas_call(
            lambda *refs: bulk_kernel(beta, first_live, cap, *refs),
            grid_spec=pltpu.PrefetchScalarGridSpec(
                num_scalar_prefetch=1,
                grid=(batches, groups),
                in_specs=[
                    pl.BlockSpec((1, nodes, width), lambda b, g, m: (b, 0, 0)),
                    pl.BlockSpec((lines, width), lambda b, g, m: (0, 0)),
                    pl.BlockSpec((1, row_tiles // groups, kt, tile, tile), lambda b, g, m: (b, g, 0, 0, 0)),
                    pl.BlockSpec((1, rows, width), lambda b, g, m: (b, g, 0)),
                    pl.BlockSpec((width, width), lambda b, g, m: (0, 0)),
                    pl.BlockSpec((1, bound, rows), lambda b, g, m: (b, 0, g)),
                    pl.BlockSpec((1, bound, width), lambda b, g, m: (b, 0, 0)),
                ],
                out_specs=[
                    pl.BlockSpec((1, rows, width), lambda b, g, m: (b, g, 0)),
                    pl.BlockSpec((1, bound, width), lambda b, g, m: (b, 0, 0)),
                ],
                scratch_shapes=[pltpu.VMEM((all_tiles, tile, width), bf16)],
            ),
            out_shape=(
                jax.ShapeDtypeStruct((batches, nodes, width), bf16),
                jax.ShapeDtypeStruct((batches, bound, width), f32),
            ),
            compiler_params=params(dimension_semantics=("arbitrary", "arbitrary")),
            cost_estimate=cost(7e9, 16e6),
            name="bulk",
        )(meta, x, recv, tile_vals, h0, w, local, picked3)
        return h, part.reshape(batches * bound, width)

    x = h0
    for layer in range(layers):
        beta = math.log(decay_scale / (layer + 1) + 1.0)
        w = weight_of(layer)
        ahead = None
        if layer + 1 < layers:
            ahead = exchanged(edge(part, recv, w, beta))
        x, part = bulk(x, recv, w, beta, layer // depth)
        recv = ahead
    return x[None]


def solution(mesh):
    placed = (
        P(None, "dom", None),
        P("section", None, None),
        P(None, "dom", None, None, None),
        P(None, "dom", None),
        P(None, "dom"),
        P(None, "dom", None),
        P(None, "dom"),
    )
    return jax.shard_map(
        body, mesh=mesh, in_specs=placed, out_specs=P("section", None, "dom", None), check_vma=False
    )
```
